1024 devices in a mesh: gx: 16 (over z), gy: 4 (over x_hi, core), gz: 16 (over x_lo, y).
Axes of the slice: x: 4 (x_hi: 2, x_lo: 2; x = x_hi * 2 + x_lo), y: 8, z: 16, core: 2. Of those that a mesh axis runs over, the one named last changes fastest.
Arguments:
- species: float32 [128, 32, 128, 256], P('gx', 'gy', 'gz'), may hold values from 0.25 to 4
- substeps: int32 [64, 4, 16], P('gx', 'gy', 'gz'), may hold values from 1 to 4, as said below
- reactants: int32 [1024, 256], replicated, may hold values from 0 to 2, as said below
- products: int32 [1024, 256], replicated, may hold values from 0 to 2, as said below
- rate_const: float32 [1024], replicated, may hold values from 0.01 to 0.2
- velocity: float32 [3, 128, 32, 128], P(None, 'gx', 'gy', 'gz'), may hold values from -0.3 to 0.3
- viscosity: float32 [128, 32, 128], P('gx', 'gy', 'gz'), may hold values from 0.25 to 1
- diffusivity: float32 [256], replicated, may hold values from 0.03 to 0.12
Outputs:
- evolved: float32 [128, 32, 128, 256], P('gx', 'gy', 'gz')
The draws below stay inside these ranges and needn't reach their ends.
Inputs may be any that keep to these rules, and one draw needn't show every extreme that they name: `substeps`: one entry for each block of 128 cells (2 x-planes of a brick); the value 4 occurs in every draw. `reactants`: each row sums to 2. `products`: each row sums to 2.
All inputs are finite; a program needn't handle non-finite values.
Results may differ from the reference program's by a relative error of at most 0.00077.
Values sent between devices are 32-bit elements; how exact they have to be, the bound alone decides.
A program may use at most 32 MiB of HBM per device.

```python
import math
import jax
import jax.numpy as jnp
from jax import lax

S = 256
R = 1024
BY = 8
BZ = 8
BLOCK = 128
MAX_SUB = 4
PLANES = 2
NX = 128
NY = 32
NZ = 128
BLK_X = 64
BLK_Y = 4
BLK_Z = 16


def draw_substeps(key, part):
    key_center = jax.random.fold_in(key, 101)
    key_flame = jax.random.fold_in(key, 202)
    key_quiet = jax.random.fold_in(key, 303)
    center = jax.random.randint(key_center, (), 0, BLK_X)
    blocks = jnp.arange(BLK_X)
    flame_mask = (blocks - center) % BLK_X < max(BLK_X // 8, 1)
    flame_counts = jax.random.randint(key_flame, (BLK_X, BLK_Y, BLK_Z), 3, 5)
    quiet_counts = jax.random.randint(key_quiet, (BLK_X, BLK_Y, BLK_Z), 1, 3)
    counts = jnp.where(flame_mask[:, None, None], flame_counts, quiet_counts)
    counts = counts.at[center, 0, 0].set(4)
    return counts.astype(jnp.int32)


def pick_matrix(key):
    slots = jax.random.randint(key, (R, 2), 0, S)
    slots = slots.at[0, 1].set(slots[0, 0])
    species_ids = jnp.arange(S)
    matrix = (slots[:, 0:1] == species_ids[None, :]).astype(jnp.int32) + (slots[:, 1:2] == species_ids[None, :]).astype(jnp.int32)
    return matrix.astype(jnp.int32)


def draw_reactants(key, part):
    return pick_matrix(jax.random.fold_in(key, 11))


def draw_products(key, part):
    return pick_matrix(jax.random.fold_in(key, 23))


def steps_of(rng, dims, pieces, smallest, top_value):
    def one(dim, parts):
        draws = jax.random.uniform(jax.random.fold_in(jax.random.fold_in(rng, 6), dim), (parts,), jnp.float32, smallest / len(pieces), top_value / len(pieces))
        return jnp.repeat(jnp.exp(draws), dims[dim] // parts).reshape((-1,) + (1,) * (len(dims) - dim - 1))

    loudness = one(*pieces[0])
    for cut in pieces[1:]:
        loudness = loudness * one(*cut)
    return loudness


def setup_inputs(seed: int = 0) -> dict:
    arg_keys = jax.random.split(jax.random.key(seed), 9)
    return {
        "species": jnp.clip(jnp.exp(math.log(4.0) - 2.7725887 * jax.random.uniform(arg_keys[0], (NX, NY, NZ, S), jnp.float32) ** steps_of(arg_keys[0], (NX, NY, NZ, S), ((0, 16), (1, 4), (2, 16)), -0.2, 0.2)), 0.25, 4.0),
        "substeps": draw_substeps(jax.random.fold_in(arg_keys[8], 71), 0),
        "reactants": draw_reactants(jax.random.fold_in(arg_keys[8], 71), 0),
        "products": draw_products(jax.random.fold_in(arg_keys[8], 71), 0),
        "rate_const": jnp.clip(jnp.exp(jax.random.uniform(arg_keys[4], (R,), jnp.float32, math.log(0.01), math.log(0.2))), 0.01, 0.2),
        "velocity": jnp.clip(jax.random.uniform(arg_keys[5], (3, NX, NY, NZ), jnp.float32, -0.3, 0.3) * steps_of(arg_keys[5], (3, NX, NY, NZ), ((1, 16), (2, 4), (3, 16)), -0.4, 0.0), -0.3, 0.3),
        "viscosity": jnp.clip(jnp.exp(math.log(1.0) - 1.3862944 * jax.random.uniform(arg_keys[6], (NX, NY, NZ), jnp.float32) ** steps_of(arg_keys[6], (NX, NY, NZ), ((0, 16), (1, 4), (2, 16)), -0.2, 0.2)), 0.25, 1.0),
        "diffusivity": jnp.clip(jnp.exp(jax.random.uniform(arg_keys[7], (S,), jnp.float32, math.log(0.03), math.log(0.12))), 0.03, 0.12),
    }


def react(conc, length, reactant_table, stoich, rate_const):
    logs = jnp.log(conc)
    expo = lax.dot_general(logs, reactant_table, (((1,), (1,)), ((), ())), precision=lax.Precision.HIGHEST, preferred_element_type=jnp.float32)
    rates = (rate_const * jnp.exp(expo)).astype(jnp.bfloat16)
    terms = jnp.dot(rates, stoich, preferred_element_type=jnp.float32)
    width = conc.shape[1]
    made = terms[:, :width]
    used = terms[:, width:]
    return conc * (conc + length * made) / (conc + length * used)


def window(array, axis, offset):
    index = []
    for place in range(3):
        shift = offset if place == axis else 0
        index.append(slice(1 + shift, array.shape[place] - 1 + shift))
    return array[tuple(index)]


def divergence(field, coef, diffusivity):
    inner = window(field, 0, 0)
    visc = window(coef[3], 0, 0)
    total = jnp.zeros(inner.shape, jnp.float32)
    for axis in range(3):
        ahead = window(field, axis, 1)
        behind = window(field, axis, -1)
        speed = window(coef[axis], 0, 0)[..., None]
        speed_behind = window(coef[axis], axis, -1)[..., None]
        visc_ahead = window(coef[3], axis, 1)
        visc_behind = window(coef[3], axis, -1)
        flux_up = speed * (inner + ahead) * 0.5 - diffusivity * ((visc + visc_ahead) * 0.5)[..., None] * (ahead - inner)
        flux_down = speed_behind * (behind + inner) * 0.5 - diffusivity * ((visc_behind + visc) * 0.5)[..., None] * (inner - behind)
        total = total - (flux_up - flux_down)
    return total


def reference(species, substeps, reactants, products, rate_const, velocity, viscosity, diffusivity):
    reactant_table = reactants.astype(jnp.float32)
    stoich = jnp.concatenate([products, reactants], axis=1).astype(jnp.bfloat16)
    cell_counts = jnp.repeat(jnp.repeat(jnp.repeat(substeps, PLANES, axis=0), BY, axis=1), BZ, axis=2)
    rows = species.reshape(-1, BLOCK, S)
    counts = cell_counts.reshape(-1, BLOCK)

    def one_block(pair):
        conc, block_counts = pair
        length = 1.0 / block_counts.astype(jnp.float32)[:, None]
        for level in range(1, MAX_SUB + 1):
            fresh = react(conc, length, reactant_table, stoich, rate_const)
            conc = jnp.where((block_counts >= level)[:, None], fresh, conc)
        return conc

    reacted = lax.map(one_block, (rows, counts)).reshape(NX, NY, NZ, S)
    coef = jnp.concatenate([velocity, viscosity[None]], axis=0)
    coef_pad = jnp.pad(coef, ((0, 0), (1, 1), (1, 1), (1, 1)), mode="wrap")

    def operate(field, diff_group):
        padded = jnp.pad(field, ((1, 1), (1, 1), (1, 1), (0, 0)), mode="wrap")
        return divergence(padded, coef_pad, diff_group)

    def heun(pair):
        field, diff_group = pair
        first = field + operate(field, diff_group)
        return 0.5 * field + 0.5 * (first + operate(first, diff_group))

    grouped = jnp.moveaxis(reacted.reshape(NX, NY, NZ, 8, S // 8), 3, 0)
    diff_groups = diffusivity.reshape(8, S // 8)
    result = lax.map(heun, (grouped, diff_groups))
    return jnp.moveaxis(result, 0, 3).reshape(NX, NY, NZ, S)
```

```python
import functools

import jax
import jax.numpy as jnp
from jax import lax
from jax.experimental import pallas as pl
from jax.experimental.pallas import tpu as pltpu
from jax.sharding import PartitionSpec as P

MESH = pl.DeviceIdType.MESH
MAX_SUB = 4
F32 = jnp.float32
BF16 = jnp.bfloat16
DIRS = (("gx", 1), ("gx", -1), ("gy", 1), ("gy", -1), ("gz", 1), ("gz", -1))


def lane_column(row, mask):
    picked = jnp.where(mask, jnp.broadcast_to(row, mask.shape), 0.0)
    return jnp.broadcast_to(jnp.sum(picked, axis=1, keepdims=True), (8, 128))


def twice(c):
    return jnp.concatenate([c, c], axis=1)


def kernel(
    sizes,
    species,
    reactants,
    products,
    counts,
    rate,
    velocity,
    viscosity,
    diffusivity,
    out,
    react_i,
    prod_i,
    table,
    stoich,
    v1,
    v2,
    pack1,
    pack2,
    z1,
    z2,
    result,
    hx,
    hy,
    hz,
    nu,
    hzm,
    nzlo,
    nzhi,
    csend,
    crecv,
    load_sem,
    out_sem,
    send_sem,
    recv_sem,
):
    def toward(k):
        axis, step = DIRS[k]
        n = sizes[axis]
        return {axis: lax.rem(lax.axis_index(axis) + (step + n), n)}

    barrier = pltpu.get_barrier_semaphore()
    for k in range(6):
        pl.semaphore_signal(barrier, inc=1, device_id=toward(k), device_id_type=MESH)

    loads = [
        pltpu.make_async_copy(reactants, react_i, load_sem.at[0]),
        pltpu.make_async_copy(species.at[pl.ds(6, 2)], v1.at[pl.ds(7, 2), pl.ds(1, 8)], load_sem.at[1]),
        pltpu.make_async_copy(products, prod_i, load_sem.at[2]),
        pltpu.make_async_copy(species.at[pl.ds(0, 6)], v1.at[pl.ds(1, 6), pl.ds(1, 8)], load_sem.at[3]),
    ]
    for copy in loads:
        copy.start()

    sub = lax.broadcasted_iota(jnp.int32, (8, 8), 0)
    lane = lax.broadcasted_iota(jnp.int32, (8, 8), 1)
    eye = sub == lane

    def expand(x, _):
        for y in range(8):
            hx[1 + x, y] = 0.5 * lane_column(velocity[0, x, y : y + 1, :], eye)
            hy[x, 1 + y] = 0.5 * lane_column(velocity[1, x, y : y + 1, :], eye)
            hz[x, y] = 0.5 * lane_column(velocity[2, x, y : y + 1, :], eye)
            nu[1 + x, 1 + y] = 0.5 * lane_column(viscosity[x, y : y + 1, :], eye)
        for k, row in ((2, 7), (3, 0)):
            csend[k, 0, pl.ds(x, 1), 0:8] = velocity[1, x, row : row + 1, :]
            csend[k, 1, pl.ds(x, 1), 0:8] = viscosity[x, row : row + 1, :]
        for k, col in ((4, 7), (5, 0)):
            for slot, tile in ((0, velocity[2, x]), (1, viscosity[x])):
                column = jnp.sum(jnp.where(lane == col, tile, 0.0), axis=1, keepdims=True)
                row = jnp.sum(jnp.where(eye, jnp.broadcast_to(column, (8, 8)), 0.0), axis=0, keepdims=True)
                csend[k, slot, pl.ds(x, 1), 0:8] = row
        return 0

    lax.fori_loop(0, 8, expand, 0)
    for k, plane in ((0, 7), (1, 0)):
        csend[k, 0, :, 0:8] = velocity[0, plane]
        csend[k, 1, :, 0:8] = viscosity[plane]

    loads[0].wait()
    rb = react_i[...].astype(F32).astype(BF16)
    table[:, 0:256] = rb
    table[:, 256:512] = rb
    stoich[:, 256:512] = rb
    loads[2].wait()
    stoich[:, 0:256] = prod_i[...].astype(F32).astype(BF16)

    def chemistry(first_block, blocks):
        rows = blocks * 128
        planes = pl.ds(1 + 2 * first_block, 2 * blocks)

        def level_step(level, _):
            conc = v1[planes, 1:9].reshape(rows, 256)
            logs = jnp.log(conc)
            high = logs.astype(BF16)
            low = (logs - high.astype(F32)).astype(BF16)
            both = jnp.concatenate([high, low], axis=1)
            expo = lax.dot_general(both, table[...], (((1,), (1,)), ((), ())), preferred_element_type=F32)
            rates = (rate[...] * jnp.exp(expo)).astype(BF16)
            terms = jnp.dot(rates, stoich[...], preferred_element_type=F32)
            for b in range(blocks):
                count = jnp.full((1, 256), counts[first_block + b], jnp.int32)
                length = 1.0 / count.astype(F32)
                part = slice(128 * b, 128 * b + 128)
                old = conc[part]
                fresh = old * (old + length * terms[part, 0:256]) / (old + length * terms[part, 256:512])
                new = jnp.where(count >= level, fresh, old)
                v1[pl.ds(1 + 2 * (first_block + b), 2), 1:9] = new.reshape(2, 8, 8, 256)
            return 0

        lax.fori_loop(1, MAX_SUB + 1, level_step, 0)

    def pack(field, packed, x):
        for y in range(8):
            packed[0, x, y : y + 1, :] = field[1 + x, 1 + y, 0:1, :]
            packed[1, x, y : y + 1, :] = field[1 + x, 1 + y, 7:8, :]

    used = []

    def message(k, src, dst):
        i = len(used)
        copy = pltpu.make_async_remote_copy(
            src_ref=src,
            dst_ref=dst,
            send_sem=send_sem.at[i],
            recv_sem=recv_sem.at[i],
            device_id=toward(k),
            device_id_type=MESH,
        )
        used.append(copy)
        copy.start()
        return copy

    def send_x(k, field):
        src, dst = (8, 0) if k == 0 else (1, 9)
        return message(k, field.at[src, pl.ds(1, 8)], field.at[dst, pl.ds(1, 8)])

    def send_yz(field, packed, halo, x0, n):
        xs, ps = pl.ds(1 + x0, n), pl.ds(x0, n)
        return [
            message(2, field.at[xs, 8], field.at[xs, 0]),
            message(3, field.at[xs, 1], field.at[xs, 9]),
            message(4, packed.at[1, ps], halo.at[0, ps]),
            message(5, packed.at[0, ps], halo.at[1, ps]),
        ]

    row8 = lax.broadcasted_iota(jnp.int32, (8, 128), 0)
    row8w = lax.broadcasted_iota(jnp.int32, (8, 256), 0)
    diff = diffusivity[...]

    def operate(field, halo, x, y):
        v = field[1 + x, 1 + y]
        n = nu[1 + x, 1 + y]
        h = hz[x, y]
        up = jnp.where(row8w == 7, halo[1, x, y : y + 1, :], pltpu.roll(v, 7, 0))
        down = jnp.where(row8w == 0, halo[0, x, y : y + 1, :], pltpu.roll(v, 1, 0))
        h_down = jnp.where(row8 == 0, hzm[x, y : y + 1, :], pltpu.roll(h, 1, 0))
        n_up = jnp.where(row8 == 7, nzhi[x, y : y + 1, :], pltpu.roll(n, 7, 0))
        n_down = jnp.where(row8 == 0, nzlo[x, y : y + 1, :], pltpu.roll(n, 1, 0))
        carried, spread = None, None
        for ahead, behind, h0, h1, n0, n1 in (
            (field[2 + x, 1 + y], field[x, 1 + y], hx[1 + x, y], hx[x, y], nu[2 + x, 1 + y], nu[x, 1 + y]),
            (field[1 + x, 2 + y], field[1 + x, y], hy[x, 1 + y], hy[x, y], nu[1 + x, 2 + y], nu[1 + x, y]),
            (up, down, h, h_down, n_up, n_down),
        ):
            flow = twice(h0) * (v + ahead) - twice(h1) * (behind + v)
            mix = twice(n + n0) * (ahead - v) - twice(n1 + n) * (v - behind)
            carried = flow if carried is None else carried + flow
            spread = mix if spread is None else spread + mix
        return v, diff * spread - carried

    def advance(x):
        for y in range(8):
            v, change = operate(v1, z1, x, y)
            v2[1 + x, 1 + y] = v + change
        pack(v2, pack2, x)

    def finish(x):
        for y in range(8):
            v, change = operate(v2, z2, x, y)
            result[x, y] = 0.5 * v1[1 + x, 1 + y] + 0.5 * (v + change)

    def each(lo, hi, body):
        def step(x, _):
            body(x)
            return 0

        lax.fori_loop(lo, hi, step, 0)

    loads[1].wait()
    chemistry(3, 1)
    each(6, 8, lambda x: pack(v1, pack1, x))
    pl.semaphore_wait(barrier, 6)
    coefs = [message(k, csend.at[k], crecv.at[k]) for k in range(6)]
    r_xup = send_x(0, v1)
    r_last = send_yz(v1, pack1, z1, 6, 2)

    loads[3].wait()
    chemistry(0, 3)
    each(0, 6, lambda x: pack(v1, pack1, x))
    r_xdown = send_x(1, v1)
    r_rest = send_yz(v1, pack1, z1, 0, 6)

    for k in (1, 2, 3, 4, 5):
        coefs[k].wait_recv()
    for i in range(8):
        hy[i, 0] = 0.5 * lane_column(crecv[2, 0, i : i + 1, 0:8], eye)
        nu[1 + i, 0] = 0.5 * lane_column(crecv[2, 1, i : i + 1, 0:8], eye)
        nu[1 + i, 9] = 0.5 * lane_column(crecv[3, 1, i : i + 1, 0:8], eye)
        nu[9, 1 + i] = 0.5 * lane_column(crecv[1, 1, i : i + 1, 0:8], eye)
        hzm[i] = 0.5 * lane_column(crecv[4, 0, i : i + 1, 0:8], eye)
        nzlo[i] = 0.5 * lane_column(crecv[4, 1, i : i + 1, 0:8], eye)
        nzhi[i] = 0.5 * lane_column(crecv[5, 1, i : i + 1, 0:8], eye)

    for copy in r_last:
        copy.wait_recv()
    r_xdown.wait_recv()
    advance(7)
    f_xup = send_x(0, v2)
    for copy in r_rest:
        copy.wait_recv()
    each(1, 7, advance)
    f_rest = send_yz(v2, pack2, z2, 1, 7)
    coefs[0].wait_recv()
    for i in range(8):
        hx[0, i] = 0.5 * lane_column(crecv[0, 0, i : i + 1, 0:8], eye)
        nu[0, 1 + i] = 0.5 * lane_column(crecv[0, 1, i : i + 1, 0:8], eye)
    r_xup.wait_recv()
    advance(0)
    f_first = send_yz(v2, pack2, z2, 0, 1)
    f_xdown = send_x(1, v2)

    for copy in f_rest:
        copy.wait_recv()
    each(1, 7, finish)
    middle = pltpu.make_async_copy(result.at[pl.ds(1, 6)], out.at[pl.ds(1, 6)], out_sem.at[0])
    middle.start()
    f_xdown.wait_recv()
    finish(7)
    final = pltpu.make_async_copy(result.at[7], out.at[7], out_sem.at[1])
    final.start()
    for copy in f_first:
        copy.wait_recv()
    f_xup.wait_recv()
    finish(0)
    initial = pltpu.make_async_copy(result.at[0], out.at[0], out_sem.at[2])
    initial.start()
    for copy in used:
        copy.wait_send()
    middle.wait()
    final.wait()
    initial.wait()


def shards(sizes, species, substeps, reactants, products, rate_const, velocity, viscosity, diffusivity):
    any_space = pl.BlockSpec(memory_space=pl.ANY)
    vmem = pl.BlockSpec(memory_space=pltpu.VMEM)
    messages = 26
    return pl.pallas_call(
        functools.partial(kernel, sizes),
        out_shape=jax.ShapeDtypeStruct(species.shape, F32),
        in_specs=[any_space] * 3 + [pl.BlockSpec(memory_space=pltpu.SMEM)] + [vmem] * 4,
        out_specs=any_space,
        scratch_shapes=[
            pltpu.VMEM((1024, 256), jnp.int32),
            pltpu.VMEM((1024, 256), jnp.int32),
            pltpu.VMEM((1024, 512), BF16),
            pltpu.VMEM((1024, 512), BF16),
            pltpu.VMEM((10, 10, 8, 256), F32),
            pltpu.VMEM((10, 10, 8, 256), F32),
            pltpu.VMEM((2, 8, 8, 256), F32),
            pltpu.VMEM((2, 8, 8, 256), F32),
            pltpu.VMEM((2, 8, 8, 256), F32),
            pltpu.VMEM((2, 8, 8, 256), F32),
            pltpu.VMEM((8, 8, 8, 256), F32),
            pltpu.VMEM((9, 8, 8, 128), F32),
            pltpu.VMEM((8, 9, 8, 128), F32),
            pltpu.VMEM((8, 8, 8, 128), F32),
            pltpu.VMEM((10, 10, 8, 128), F32),
            pltpu.VMEM((8, 8, 128), F32),
            pltpu.VMEM((8, 8, 128), F32),
            pltpu.VMEM((8, 8, 128), F32),
            pltpu.VMEM((6, 2, 8, 128), F32),
            pltpu.VMEM((6, 2, 8, 128), F32),
            pltpu.SemaphoreType.DMA((4,)),
            pltpu.SemaphoreType.DMA((3,)),
            pltpu.SemaphoreType.DMA((messages,)),
            pltpu.SemaphoreType.DMA((messages,)),
        ],
        compiler_params=pltpu.CompilerParams(
            collective_id=0, has_side_effects=True, vmem_limit_bytes=63 * 2**20
        ),
    )(
        species,
        reactants,
        products,
        substeps.reshape(-1),
        rate_const.reshape(1, -1),
        velocity,
        viscosity,
        diffusivity.reshape(1, -1),
    )


def solution(mesh):
    return jax.shard_map(
        functools.partial(shards, dict(mesh.shape)),
        mesh=mesh,
        in_specs=(
            P("gx", "gy", "gz", None),
            P("gx", "gy", "gz"),
            P(),
            P(),
            P(),
            P(None, "gx", "gy", "gz"),
            P("gx", "gy", "gz"),
            P(),
        ),
        out_specs=P("gx", "gy", "gz", None),
        check_vma=False,
    )
```

```python
import functools

import jax
import jax.numpy as jnp
from jax import lax
from jax.experimental import pallas as pl
from jax.experimental.pallas import tpu as pltpu
from jax.sharding import PartitionSpec as P

MESH = pl.DeviceIdType.MESH
MAX_SUB = 4
F32 = jnp.float32
BF16 = jnp.bfloat16
AXES = ("gx", "gy", "gz")
FACES = ((1, 0, 0), (-1, 0, 0), (0, 1, 0), (0, -1, 0), (0, 0, 1), (0, 0, -1))
EDGES = tuple((a, b, 0) for a in (1, -1) for b in (1, -1))
EDGES += tuple((a, 0, c) for a in (1, -1) for c in (1, -1))
EDGES += tuple((0, b, c) for b in (1, -1) for c in (1, -1))
AHEAD = tuple(s for s in FACES + EDGES if s[0] == 1)
GREETED = tuple(s for s in FACES + EDGES if s[0] != 1)


def twice(c):
    return jnp.concatenate([c, c], axis=1)


def kernel(
    sizes,
    species,
    reactants,
    products,
    substeps,
    rate_const,
    velocity,
    viscosity,
    diffusivity,
    out,
    react_i,
    prod_i,
    counts,
    rate,
    coef,
    diff_ref,
    table,
    stoich,
    v1,
    v2,
    zp,
    zf,
    yzp,
    yz,
    z2,
    k1,
    kzp,
    kx,
    ky,
    kz,
    kyz,
    kx_in,
    ky_in,
    kz_in,
    ke_in,
    kyz_in,
    spread,
    zspread,
    yzspread,
    result,
    load_sem,
    out_sem,
    send_sem,
    recv_sem,
    entry_sem,
):
    def toward(steps):
        place = {}
        for axis, step in zip(AXES, steps):
            if step:
                n = sizes[axis]
                place[axis] = lax.rem(lax.axis_index(axis) + (step + n), n)
        return place

    barrier = pltpu.get_barrier_semaphore()
    for steps in GREETED:
        pl.semaphore_signal(barrier, inc=1, device_id=toward(steps), device_id_type=MESH)

    loads = []
    for src, dst in (
        (reactants, react_i),
        (species.at[pl.ds(6, 2)], v1.at[pl.ds(8, 2), pl.ds(2, 8)]),
        (rate_const, rate),
        (substeps, counts),
        (products, prod_i),
        (species.at[pl.ds(0, 6)], v1.at[pl.ds(2, 6), pl.ds(2, 8)]),
        (velocity, coef.at[pl.ds(0, 3)]),
        (viscosity, coef.at[3]),
        (diffusivity, diff_ref),
    ):
        copy = pltpu.make_async_copy(src, dst, load_sem.at[len(loads)])
        copy.start()
        loads.append(copy)

    eye = lax.broadcasted_iota(jnp.int32, (8, 8), 0) == lax.broadcasted_iota(jnp.int32, (8, 8), 1)
    row = lax.broadcasted_iota(jnp.int32, (8, 128), 0)
    row_wide = lax.broadcasted_iota(jnp.int32, (8, 256), 0)
    lane = lax.broadcasted_iota(jnp.int32, (8, 128), 1)
    kind, place = lax.rem(lane, 4), lane // 4

    def each(lo, hi, body):
        def step(x, _):
            body(x)
            return 0

        lax.fori_loop(lo, hi, step, 0)

    def pack_z(field, base, packed, x):
        for layer, z in enumerate((0, 1, 6, 7)):
            for y in range(8):
                packed[layer, x, y : y + 1, :] = field[base + x, base + y, z : z + 1, :]

    def pack_yz(field, base, packed):
        for i, (y, z) in enumerate(((7, 7), (7, 0), (0, 7), (0, 0))):
            for x in range(8):
                packed[i, x : x + 1, :] = field[base + x, base + y, z : z + 1, :]

    used = []

    def message(steps, src, dst):
        i = len(used)
        copy = pltpu.make_async_remote_copy(
            src_ref=src,
            dst_ref=dst,
            send_sem=send_sem.at[i],
            recv_sem=recv_sem.at[i],
            device_id=toward(steps),
            device_id_type=MESH,
        )
        used.append(copy)
        return copy

    def start(copies):
        for copy in copies:
            copy.start()
        return copies

    own = pl.ds(2, 8)

    def send_plus(field, packed, halo):
        n = 2
        copies = [message((1, 0, 0), field.at[pl.ds(8, n), own], field.at[pl.ds(0, n), own])]
        copies.append(message((1, 1, 0), field.at[9, 9], field.at[1, 1]))
        copies.append(message((1, -1, 0), field.at[9, 2], field.at[1, 10]))
        copies.append(message((1, 0, 1), packed.at[3, 7], halo.at[1, 0]))
        copies.append(message((1, 0, -1), packed.at[0, 7], halo.at[2, 0]))
        return copies

    def send_minus(field, packed, halo):
        copies = [message((-1, 0, 0), field.at[pl.ds(2, 2), own], field.at[pl.ds(10, 2), own])]
        copies.append(message((-1, 1, 0), field.at[2, 9], field.at[10, 1]))
        copies.append(message((-1, -1, 0), field.at[2, 2], field.at[10, 10]))
        copies.append(message((-1, 0, 1), packed.at[3, 0], halo.at[1, 9]))
        copies.append(message((-1, 0, -1), packed.at[0, 0], halo.at[2, 9]))
        return copies

    def send_side(field, packed, halo, edges, edge_halo):
        mid = pl.ds(1, 8)
        lo, hi = pl.ds(0, 2), pl.ds(2, 2)
        copies = [
            message((0, 1, 0), field.at[own, pl.ds(8, 2)], field.at[own, pl.ds(0, 2)]),
            message((0, -1, 0), field.at[own, pl.ds(2, 2)], field.at[own, pl.ds(10, 2)]),
            message((0, 0, 1), packed.at[hi], halo.at[lo, mid]),
            message((0, 0, -1), packed.at[lo], halo.at[hi, mid]),
        ]
        for i, steps in enumerate(EDGES[8:]):
            copies.append(message(steps, edges.at[i], edge_halo.at[i]))
        return copies

    def widen(tile, place):
        at = 4 * place
        return [jnp.broadcast_to(tile[:, at + c : at + c + 1], (8, 128)) for c in range(4)]

    def own_coefficients(x):
        rows_x = None
        for y in range(8):
            merged = None
            for c in range(4):
                line = coef[c, x, y : y + 1, :]
                picked = jnp.where(eye, jnp.broadcast_to(line, (8, 8)), 0.0)
                column = jnp.broadcast_to(0.5 * jnp.sum(picked, axis=1, keepdims=True), (8, 128))
                spread[2 + x, 2 + y, c] = column
                merged = column if c == 0 else jnp.where(kind == c, column, merged)
            k1[x, y] = merged
            rows_x = merged if y == 0 else jnp.where(place == y, merged, rows_x)
            ky[y] = jnp.where(place == x, merged, ky[y])
        kx[x] = rows_x
        pack_z(k1, 0, kzp, x)
        for layer in range(4):
            kz[layer] = jnp.where(place == x, kzp[layer, x], kz[layer])
        for layer, clayer in ((0, 2), (3, 3)):
            for c, value in enumerate(widen(kzp[layer, x], 0)):
                zspread[clayer, 1 + x, c] = value

    def send_coefficients():
        pack_yz(k1, 0, kyz)
        lo, hi = pl.ds(0, 2), pl.ds(6, 2)
        plus = [message((1, 0, 0), kx.at[hi], kx_in.at[0])]
        plus.append(message((1, 1, 0), kx.at[7], ke_in.at[0]))
        plus.append(message((1, -1, 0), kx.at[7], ke_in.at[1]))
        plus.append(message((1, 0, 1), kz.at[3], ke_in.at[4]))
        plus.append(message((1, 0, -1), kz.at[0], ke_in.at[5]))
        minus = [message((-1, 0, 0), kx.at[lo], kx_in.at[1])]
        minus.append(message((-1, 1, 0), kx.at[0], ke_in.at[2]))
        minus.append(message((-1, -1, 0), kx.at[0], ke_in.at[3]))
        minus.append(message((-1, 0, 1), kz.at[3], ke_in.at[6]))
        minus.append(message((-1, 0, -1), kz.at[0], ke_in.at[7]))
        side = [message((0, 1, 0), ky.at[hi], ky_in.at[0])]
        side.append(message((0, -1, 0), ky.at[lo], ky_in.at[1]))
        side.append(message((0, 0, 1), kz.at[pl.ds(2, 2)], kz_in.at[0]))
        side.append(message((0, 0, -1), kz.at[lo], kz_in.at[1]))
        for i, steps in enumerate(EDGES[8:]):
            side.append(message(steps, kyz.at[i], kyz_in.at[i]))
        return start(plus), minus, start(side)

    loads[0].wait()
    rb = react_i[...].astype(F32).astype(BF16)
    table[:, 0:256] = rb
    table[:, 256:512] = rb
    stoich[:, 256:512] = rb
    for i in (1, 2, 3, 4):
        loads[i].wait()
    stoich[:, 0:256] = prod_i[...].astype(F32).astype(BF16)

    def chemistry(first_block, blocks, from_level, to_level, beside=None):
        rows = blocks * 128
        planes = pl.ds(2 + 2 * first_block, 2 * blocks)

        def level_step(level, _):
            conc = v1[planes, 2:10].reshape(rows, 256)
            logs = jnp.log(conc)
            high = logs.astype(BF16)
            low = (logs - high.astype(F32)).astype(BF16)
            both = jnp.concatenate([high, low], axis=1)
            if beside is not None:
                beside(level)
            expo = lax.dot_general(both, table[...], (((1,), (1,)), ((), ())), preferred_element_type=F32)
            rates = (rate[...] * jnp.exp(expo)).astype(BF16)
            terms = jnp.dot(rates, stoich[...], preferred_element_type=F32)
            for b in range(blocks):
                count = jnp.full((1, 256), counts[first_block + b], jnp.int32)
                length = 1.0 / count.astype(F32)
                part = slice(128 * b, 128 * b + 128)
                old = conc[part]
                fresh = old * (old + length * terms[part, 0:256]) / (old + length * terms[part, 256:512])
                new = jnp.where(count >= level, fresh, old)
                v1[pl.ds(2 + 2 * (first_block + b), 2), 2:10] = new.reshape(2, 8, 8, 256)
            return 0

        lax.fori_loop(from_level, to_level + 1, level_step, 0)

    def flux(diff, v, n, parts):
        carried, mixed = None, None
        for ahead, behind, h0, h1, n0, n1 in parts:
            flow = twice(h0) * (v + ahead) - twice(h1) * (behind + v)
            mix = twice(n + n0) * (ahead - v) - twice(n1 + n) * (v - behind)
            carried = flow if carried is None else carried + flow
            mixed = mix if mixed is None else mixed + mix
        return diff * mixed - carried

    def shift(value, rows, below, above):
        up = jnp.where(rows == 7, above, pltpu.roll(value, 7, 0))
        down = jnp.where(rows == 0, below, pltpu.roll(value, 1, 0))
        return up, down

    def column(field, base, x, y, below, above, coef_below, coef_above):
        fx, fy, cx, cy = x + base, y + base, x + 2, y + 2
        v, n, h = field[fx, fy], spread[cx, cy, 3], spread[cx, cy, 2]
        up, down = shift(v, row_wide, below, above)
        n_up, n_down = shift(n, row, coef_below(3), coef_above(3))
        h_down = jnp.where(row == 0, coef_below(2), pltpu.roll(h, 1, 0))
        parts = (
            (field[fx + 1, fy], field[fx - 1, fy], spread[cx, cy, 0], spread[cx - 1, cy, 0], spread[cx + 1, cy, 3], spread[cx - 1, cy, 3]),
            (field[fx, fy + 1], field[fx, fy - 1], spread[cx, cy, 1], spread[cx, cy - 1, 1], spread[cx, cy + 1, 3], spread[cx, cy - 1, 3]),
            (up, down, h, h_down, n_up, n_down),
        )
        return v, flux(diff_ref[...], v, n, parts)

    def zcoef(layer, x, y):
        return lambda c: zspread[layer, 1 + x, c, y : y + 1, :]

    def yzcoef(i, x):
        return lambda c: yzspread[i, c, pl.ds(x, 1), :]

    def first_plane(x):
        for y in range(8):
            below, above = zf[1, 1 + x, y : y + 1, :], zf[2, 1 + x, y : y + 1, :]
            v, change = column(v1, 2, x, y, below, above, zcoef(1, x, y), zcoef(4, x, y))
            v2[1 + x, 1 + y] = v + change

    def first_rim(x):
        for y, i, j in ((-1, 0, 1), (8, 2, 3)):
            below, above = yz[i, pl.ds(x, 1), :], yz[j, pl.ds(x, 1), :]
            v, change = column(v1, 2, x, y, below, above, yzcoef(i, x), yzcoef(j, x))
            v2[1 + x, 1 + y] = v + change
        for side, layer, clayer, i, j in ((0, 1, 1, 0, 2), (1, 2, 4, 1, 3)):
            v, n, h = zf[layer, 1 + x], zspread[clayer, 1 + x, 3], zspread[clayer, 1 + x, 1]
            up, down = shift(v, row_wide, yz[i, pl.ds(x, 1), :], yz[j, pl.ds(x, 1), :])
            n_up, n_down = shift(n, row, yzcoef(i, x)(3), yzcoef(j, x)(3))
            h_down = jnp.where(row == 0, yzcoef(i, x)(1), pltpu.roll(h, 1, 0))
            ahead = zp[0, x] if side == 0 else zf[3, 1 + x]
            behind = zf[0, 1 + x] if side == 0 else zp[3, x]
            c = 1 + x
            parts = (
                (zf[layer, c + 1], zf[layer, c - 1], zspread[clayer, c, 0], zspread[clayer, c - 1, 0], zspread[clayer, c + 1, 3], zspread[clayer, c - 1, 3]),
                (up, down, h, h_down, n_up, n_down),
                (ahead, behind, zspread[clayer, c, 2], zspread[clayer - 1, c, 2], zspread[clayer + 1, c, 3], zspread[clayer - 1, c, 3]),
            )
            z2[side, x] = v + flux(diff_ref[...], v, n, parts)

    def finish(x):
        for y in range(8):
            below, above = z2[0, x, y : y + 1, :], z2[1, x, y : y + 1, :]
            v, change = column(v2, 1, x, y, below, above, zcoef(1, x, y), zcoef(4, x, y))
            result[x, y] = 0.5 * v1[2 + x, 2 + y] + 0.5 * (v + change)

    def widen_column(x, y, tile, at):
        for c, value in enumerate(widen(tile, at)):
            spread[2 + x, 2 + y, c] = value

    def widen_layer(clayer, x, tile, at):
        for c, value in enumerate(widen(tile, at)):
            zspread[clayer, 1 + x, c] = value

    def widen_plane(side, places, x, edges, at):
        for i, place_x in enumerate(places):
            tile = kx_in[side, i]
            for y in range(8):
                widen_column(place_x, y, tile, y)
        widen_column(x, -1, ke_in[edges], 7)
        widen_column(x, 8, ke_in[edges + 1], 0)
        widen_layer(1, x, ke_in[4 + edges], at)
        widen_layer(4, x, ke_in[5 + edges], at)

    def widen_sides():
        for side, i, y in ((0, 0, -2), (0, 1, -1), (1, 0, 8), (1, 1, 9)):
            tile = ky_in[side, i]
            for x in range(8):
                widen_column(x, y, tile, x)
        for side, i, clayer in ((0, 0, 0), (0, 1, 1), (1, 0, 4), (1, 1, 5)):
            tile = kz_in[side, i]
            for x in range(8):
                widen_layer(clayer, x, tile, x)
        for i in range(4):
            for c, value in enumerate(widen(kyz_in[i], 0)):
                yzspread[i, c] = value

    def store(i, x, n):
        copy = pltpu.make_async_copy(result.at[pl.ds(x, n)], out.at[pl.ds(x, n)], out_sem.at[i])
        copy.start()
        return copy

    ky[...] = jnp.zeros_like(ky)
    kz[...] = jnp.zeros_like(kz)
    for i in (6, 7, 8):
        loads[i].wait()

    def two_planes(level):
        own_coefficients(2 * level - 2)
        own_coefficients(2 * level - 1)

    chemistry(3, 1, 1, 2, two_planes)
    pl.semaphore_wait(barrier, len(GREETED))
    for steps in AHEAD:
        pl.semaphore_signal(entry_sem, inc=1, device_id=toward(steps), device_id_type=MESH)
    chemistry(3, 1, 3, MAX_SUB, two_planes)
    each(6, 8, lambda x: pack_z(v1, 2, zp, x))
    r_plus = start(send_plus(v1, zp, zf))
    k_plus, k_minus, k_side = send_coefficients()

    loads[5].wait()
    chemistry(0, 3, 1, MAX_SUB)
    each(0, 6, lambda x: pack_z(v1, 2, zp, x))
    pack_yz(v1, 2, yzp)
    r_side = start(send_side(v1, zp, zf, yzp, yz))
    r_minus = send_minus(v1, zp, zf)

    first_along = lax.axis_index("gx") == 0

    def send_back():
        pl.semaphore_wait(entry_sem, len(AHEAD))
        start(k_minus)
        start(r_minus)

    pl.when(jnp.logical_not(first_along))(send_back)

    for copy in k_side:
        copy.wait_recv()
    widen_sides()
    for copy in r_side:
        copy.wait_recv()
    each(1, 7, first_plane)
    each(1, 7, first_rim)
    each(2, 6, finish)
    stored = [store(0, 2, 4)]
    for copy in k_minus:
        copy.wait_recv()
    widen_plane(1, (8, 9), 8, 2, 0)
    for copy in r_minus:
        copy.wait_recv()
    each(7, 9, first_plane)
    first_rim(7)
    each(6, 8, finish)
    stored.append(store(1, 6, 2))

    pl.when(first_along)(send_back)
    for copy in k_plus:
        copy.wait_recv()
    widen_plane(0, (-2, -1), -1, 0, 7)
    for copy in r_plus:
        copy.wait_recv()
    first_plane(-1)
    first_plane(0)
    first_rim(0)
    each(0, 2, finish)
    stored.append(store(2, 0, 2))
    for copy in used:
        copy.wait_send()
    for copy in stored:
        copy.wait()


def shards(sizes, species, substeps, reactants, products, rate_const, velocity, viscosity, diffusivity):
    hbm = pl.BlockSpec(memory_space=pltpu.HBM)
    messages = 36
    return pl.pallas_call(
        functools.partial(kernel, sizes),
        out_shape=jax.ShapeDtypeStruct(species.shape, F32),
        in_specs=[hbm] * 8,
        out_specs=hbm,
        scratch_shapes=[
            pltpu.VMEM((1024, 256), jnp.int32),
            pltpu.VMEM((1024, 256), jnp.int32),
            pltpu.SMEM((4,), jnp.int32),
            pltpu.VMEM((1, 1024), F32),
            pltpu.VMEM((4, 8, 8, 8), F32),
            pltpu.VMEM((1, 256), F32),
            pltpu.VMEM((1024, 512), BF16),
            pltpu.VMEM((1024, 512), BF16),
            pltpu.VMEM((12, 12, 8, 256), F32),
            pltpu.VMEM((10, 10, 8, 256), F32),
            pltpu.VMEM((4, 8, 8, 256), F32),
            pltpu.VMEM((4, 10, 8, 256), F32),
            pltpu.VMEM((4, 8, 256), F32),
            pltpu.VMEM((4, 8, 256), F32),
            pltpu.VMEM((2, 8, 8, 256), F32),
            pltpu.VMEM((8, 8, 8, 128), F32),
            pltpu.VMEM((4, 8, 8, 128), F32),
            pltpu.VMEM((8, 8, 128), F32),
            pltpu.VMEM((8, 8, 128), F32),
            pltpu.VMEM((4, 8, 128), F32),
            pltpu.VMEM((4, 8, 128), F32),
            pltpu.VMEM((2, 2, 8, 128), F32),
            pltpu.VMEM((2, 2, 8, 128), F32),
            pltpu.VMEM((2, 2, 8, 128), F32),
            pltpu.VMEM((8, 8, 128), F32),
            pltpu.VMEM((4, 8, 128), F32),
            pltpu.VMEM((12, 12, 4, 8, 128), F32),
            pltpu.VMEM((6, 10, 4, 8, 128), F32),
            pltpu.VMEM((4, 4, 8, 128), F32),
            pltpu.VMEM((8, 8, 8, 256), F32),
            pltpu.SemaphoreType.DMA((9,)),
            pltpu.SemaphoreType.DMA((3,)),
            pltpu.SemaphoreType.DMA((messages,)),
            pltpu.SemaphoreType.DMA((messages,)),
            pltpu.SemaphoreType.REGULAR,
        ],
        compiler_params=pltpu.CompilerParams(
            collective_id=0, has_side_effects=True, vmem_limit_bytes=63 * 2**20
        ),
    )(
        species,
        reactants,
        products,
        substeps.reshape(-1),
        rate_const.reshape(1, -1),
        velocity,
        viscosity,
        diffusivity.reshape(1, -1),
    )


def solution(mesh):
    return jax.shard_map(
        functools.partial(shards, dict(mesh.shape)),
        mesh=mesh,
        in_specs=(
            P("gx", "gy", "gz", None),
            P("gx", "gy", "gz"),
            P(),
            P(),
            P(),
            P(None, "gx", "gy", "gz"),
            P("gx", "gy", "gz"),
            P(),
        ),
        out_specs=P("gx", "gy", "gz", None),
        check_vma=False,
    )
```

```python
import functools

import jax
import jax.numpy as jnp
from jax import lax
from jax.experimental import pallas as pl
from jax.experimental.pallas import tpu as pltpu
from jax.sharding import PartitionSpec as P

MESH = pl.DeviceIdType.MESH
MAX_SUB = 4
F32 = jnp.float32
BF16 = jnp.bfloat16
AXES = ("gx", "gy", "gz")
FACES = ((1, 0, 0), (-1, 0, 0), (0, 1, 0), (0, -1, 0), (0, 0, 1), (0, 0, -1))
EDGES = tuple((a, b, 0) for a in (1, -1) for b in (1, -1))
EDGES += tuple((a, 0, c) for a in (1, -1) for c in (1, -1))
EDGES += tuple((0, b, c) for b in (1, -1) for c in (1, -1))
AHEAD = tuple(s for s in FACES + EDGES if s[0] == 1)
GREETED = tuple(s for s in FACES + EDGES if s[0] != 1)


def twice(c):
    return jnp.concatenate([c, c], axis=1)


def kernel(
    sizes,
    species,
    reactants,
    products,
    substeps,
    rate_const,
    velocity,
    viscosity,
    diffusivity,
    out,
    react_i,
    prod_i,
    counts,
    rate,
    coef,
    diff_ref,
    table,
    stoich,
    v1,
    v2,
    zp,
    zf,
    yzp,
    yz,
    z2,
    k1,
    kzp,
    kx,
    ky,
    kz,
    kyz,
    kx_in,
    ky_in,
    kz_in,
    ke_in,
    kyz_in,
    spread,
    zspread,
    yzspread,
    result,
    load_sem,
    out_sem,
    send_sem,
    recv_sem,
    entry_sem,
):
    def toward(steps):
        place = {}
        for axis, step in zip(AXES, steps):
            if step:
                n = sizes[axis]
                place[axis] = lax.rem(lax.axis_index(axis) + (step + n), n)
        return place

    barrier = pltpu.get_barrier_semaphore()
    for steps in GREETED:
        pl.semaphore_signal(barrier, inc=1, device_id=toward(steps), device_id_type=MESH)

    loads = []
    for src, dst in (
        (reactants, react_i),
        (species.at[pl.ds(6, 2)], v1.at[pl.ds(8, 2), pl.ds(2, 8)]),
        (rate_const, rate),
        (substeps, counts),
        (products, prod_i),
        (species.at[pl.ds(0, 6)], v1.at[pl.ds(2, 6), pl.ds(2, 8)]),
        (velocity, coef.at[pl.ds(0, 3)]),
        (viscosity, coef.at[3]),
        (diffusivity, diff_ref),
    ):
        copy = pltpu.make_async_copy(src, dst, load_sem.at[len(loads)])
        copy.start()
        loads.append(copy)

    eye = lax.broadcasted_iota(jnp.int32, (8, 8), 0) == lax.broadcasted_iota(jnp.int32, (8, 8), 1)
    row = lax.broadcasted_iota(jnp.int32, (8, 128), 0)
    row_wide = lax.broadcasted_iota(jnp.int32, (8, 256), 0)
    lane = lax.broadcasted_iota(jnp.int32, (8, 128), 1)
    kind, place = lax.rem(lane, 4), lane // 4

    def each(lo, hi, body):
        def step(x, _):
            body(x)
            return 0

        lax.fori_loop(lo, hi, step, 0)

    def pack_z(field, base, packed, x):
        for layer, z in enumerate((0, 1, 6, 7)):
            for y in range(8):
                packed[layer, x, y : y + 1, :] = field[base + x, base + y, z : z + 1, :]

    def pack_yz(field, base, packed):
        for i, (y, z) in enumerate(((7, 7), (7, 0), (0, 7), (0, 0))):
            for x in range(8):
                packed[i, x : x + 1, :] = field[base + x, base + y, z : z + 1, :]

    used = []

    def message(steps, src, dst):
        i = len(used)
        copy = pltpu.make_async_remote_copy(
            src_ref=src,
            dst_ref=dst,
            send_sem=send_sem.at[i],
            recv_sem=recv_sem.at[i],
            device_id=toward(steps),
            device_id_type=MESH,
        )
        used.append(copy)
        return copy

    def start(copies):
        for copy in copies:
            copy.start()
        return copies

    own = pl.ds(2, 8)

    def send_plus(field, packed, halo):
        n = 2
        copies = [message((1, 0, 0), field.at[pl.ds(8, n), own], field.at[pl.ds(0, n), own])]
        copies.append(message((1, 1, 0), field.at[9, 9], field.at[1, 1]))
        copies.append(message((1, -1, 0), field.at[9, 2], field.at[1, 10]))
        copies.append(message((1, 0, 1), packed.at[3, 7], halo.at[1, 0]))
        copies.append(message((1, 0, -1), packed.at[0, 7], halo.at[2, 0]))
        return copies

    def send_minus(field, packed, halo):
        copies = [message((-1, 0, 0), field.at[pl.ds(2, 2), own], field.at[pl.ds(10, 2), own])]
        copies.append(message((-1, 1, 0), field.at[2, 9], field.at[10, 1]))
        copies.append(message((-1, -1, 0), field.at[2, 2], field.at[10, 10]))
        copies.append(message((-1, 0, 1), packed.at[3, 0], halo.at[1, 9]))
        copies.append(message((-1, 0, -1), packed.at[0, 0], halo.at[2, 9]))
        return copies

    def send_side(field, packed, halo, edges, edge_halo):
        mid = pl.ds(1, 8)
        lo, hi = pl.ds(0, 2), pl.ds(2, 2)
        copies = [
            message((0, 1, 0), field.at[own, pl.ds(8, 2)], field.at[own, pl.ds(0, 2)]),
            message((0, -1, 0), field.at[own, pl.ds(2, 2)], field.at[own, pl.ds(10, 2)]),
            message((0, 0, 1), packed.at[hi], halo.at[lo, mid]),
            message((0, 0, -1), packed.at[lo], halo.at[hi, mid]),
        ]
        for i, steps in enumerate(EDGES[8:]):
            copies.append(message(steps, edges.at[i], edge_halo.at[i]))
        return copies

    def widen(tile, place):
        at = 4 * place
        return [jnp.broadcast_to(tile[:, at + c : at + c + 1], (8, 128)) for c in range(4)]

    def own_coefficients(x):
        rows_x = None
        for y in range(8):
            merged = None
            for c in range(4):
                line = coef[c, x, y : y + 1, :]
                picked = jnp.where(eye, jnp.broadcast_to(line, (8, 8)), 0.0)
                column = jnp.broadcast_to(0.5 * jnp.sum(picked, axis=1, keepdims=True), (8, 128))
                spread[2 + x, 2 + y, c] = column
                merged = column if c == 0 else jnp.where(kind == c, column, merged)
            k1[x, y] = merged
            rows_x = merged if y == 0 else jnp.where(place == y, merged, rows_x)
            ky[y] = jnp.where(place == x, merged, ky[y])
        kx[x] = rows_x
        pack_z(k1, 0, kzp, x)
        for layer in range(4):
            kz[layer] = jnp.where(place == x, kzp[layer, x], kz[layer])
        for layer, clayer in ((0, 2), (3, 3)):
            for c, value in enumerate(widen(kzp[layer, x], 0)):
                zspread[clayer, 1 + x, c] = value

    def send_coefficients():
        pack_yz(k1, 0, kyz)
        lo, hi = pl.ds(0, 2), pl.ds(6, 2)
        plus = [message((1, 0, 0), kx.at[hi], kx_in.at[0])]
        plus.append(message((1, 1, 0), kx.at[7], ke_in.at[0]))
        plus.append(message((1, -1, 0), kx.at[7], ke_in.at[1]))
        plus.append(message((1, 0, 1), kz.at[3], ke_in.at[4]))
        plus.append(message((1, 0, -1), kz.at[0], ke_in.at[5]))
        minus = [message((-1, 0, 0), kx.at[lo], kx_in.at[1])]
        minus.append(message((-1, 1, 0), kx.at[0], ke_in.at[2]))
        minus.append(message((-1, -1, 0), kx.at[0], ke_in.at[3]))
        minus.append(message((-1, 0, 1), kz.at[3], ke_in.at[6]))
        minus.append(message((-1, 0, -1), kz.at[0], ke_in.at[7]))
        side = [message((0, 1, 0), ky.at[hi], ky_in.at[0])]
        side.append(message((0, -1, 0), ky.at[lo], ky_in.at[1]))
        side.append(message((0, 0, 1), kz.at[pl.ds(2, 2)], kz_in.at[0]))
        side.append(message((0, 0, -1), kz.at[lo], kz_in.at[1]))
        for i, steps in enumerate(EDGES[8:]):
            side.append(message(steps, kyz.at[i], kyz_in.at[i]))
        return start(plus), minus, start(side)

    loads[0].wait()
    rb = react_i[...].astype(F32).astype(BF16)
    table[:, 0:256] = rb
    table[:, 256:512] = rb
    stoich[:, 256:512] = rb
    for i in (1, 2, 3, 4):
        loads[i].wait()
    stoich[:, 0:256] = prod_i[...].astype(F32).astype(BF16)

    def chemistry(first_block, blocks, from_level, to_level, beside=None):
        rows = blocks * 128
        planes = pl.ds(2 + 2 * first_block, 2 * blocks)

        def level_step(level, _):
            conc = v1[planes, 2:10].reshape(rows, 256)
            logs = jnp.log(conc)
            high = logs.astype(BF16)
            low = (logs - high.astype(F32)).astype(BF16)
            both = jnp.concatenate([high, low], axis=1)
            if beside is not None:
                beside(level)
            expo = lax.dot_general(both, table[...], (((1,), (1,)), ((), ())), preferred_element_type=F32)
            rates = (rate[...] * jnp.exp(expo)).astype(BF16)
            terms = jnp.dot(rates, stoich[...], preferred_element_type=F32)
            for b in range(blocks):
                count = jnp.full((1, 256), counts[first_block + b], jnp.int32)
                length = 1.0 / count.astype(F32)
                part = slice(128 * b, 128 * b + 128)
                old = conc[part]
                fresh = old * (old + length * terms[part, 0:256]) / (old + length * terms[part, 256:512])
                new = jnp.where(count >= level, fresh, old)
                v1[pl.ds(2 + 2 * (first_block + b), 2), 2:10] = new.reshape(2, 8, 8, 256)
            return 0

        lax.fori_loop(from_level, to_level + 1, level_step, 0)

    def flux(diff, v, n, parts):
        carried, mixed = None, None
        for ahead, behind, h0, h1, n0, n1 in parts:
            flow = twice(h0) * (v + ahead) - twice(h1) * (behind + v)
            mix = twice(n + n0) * (ahead - v) - twice(n1 + n) * (v - behind)
            carried = flow if carried is None else carried + flow
            mixed = mix if mixed is None else mixed + mix
        return diff * mixed - carried

    def shift(value, rows, below, above):
        up = jnp.where(rows == 7, above, pltpu.roll(value, 7, 0))
        down = jnp.where(rows == 0, below, pltpu.roll(value, 1, 0))
        return up, down

    def column(field, base, x, y, below, above, coef_below, coef_above):
        fx, fy, cx, cy = x + base, y + base, x + 2, y + 2
        v, n, h = field[fx, fy], spread[cx, cy, 3], spread[cx, cy, 2]
        up, down = shift(v, row_wide, below, above)
        n_up, n_down = shift(n, row, coef_below(3), coef_above(3))
        h_down = jnp.where(row == 0, coef_below(2), pltpu.roll(h, 1, 0))
        parts = (
            (field[fx + 1, fy], field[fx - 1, fy], spread[cx, cy, 0], spread[cx - 1, cy, 0], spread[cx + 1, cy, 3], spread[cx - 1, cy, 3]),
            (field[fx, fy + 1], field[fx, fy - 1], spread[cx, cy, 1], spread[cx, cy - 1, 1], spread[cx, cy + 1, 3], spread[cx, cy - 1, 3]),
            (up, down, h, h_down, n_up, n_down),
        )
        return v, flux(diff_ref[...], v, n, parts)

    def zcoef(layer, x, y):
        return lambda c: zspread[layer, 1 + x, c, y : y + 1, :]

    def yzcoef(i, x):
        return lambda c: yzspread[i, c, pl.ds(x, 1), :]

    def first_plane(x):
        for y in range(8):
            below, above = zf[1, 1 + x, y : y + 1, :], zf[2, 1 + x, y : y + 1, :]
            v, change = column(v1, 2, x, y, below, above, zcoef(1, x, y), zcoef(4, x, y))
            v2[1 + x, 1 + y] = v + change

    def first_rim(x):
        for y, i, j in ((-1, 0, 1), (8, 2, 3)):
            below, above = yz[i, pl.ds(x, 1), :], yz[j, pl.ds(x, 1), :]
            v, change = column(v1, 2, x, y, below, above, yzcoef(i, x), yzcoef(j, x))
            v2[1 + x, 1 + y] = v + change
        for side, layer, clayer, i, j in ((0, 1, 1, 0, 2), (1, 2, 4, 1, 3)):
            v, n, h = zf[layer, 1 + x], zspread[clayer, 1 + x, 3], zspread[clayer, 1 + x, 1]
            up, down = shift(v, row_wide, yz[i, pl.ds(x, 1), :], yz[j, pl.ds(x, 1), :])
            n_up, n_down = shift(n, row, yzcoef(i, x)(3), yzcoef(j, x)(3))
            h_down = jnp.where(row == 0, yzcoef(i, x)(1), pltpu.roll(h, 1, 0))
            ahead = zp[0, x] if side == 0 else zf[3, 1 + x]
            behind = zf[0, 1 + x] if side == 0 else zp[3, x]
            c = 1 + x
            parts = (
                (zf[layer, c + 1], zf[layer, c - 1], zspread[clayer, c, 0], zspread[clayer, c - 1, 0], zspread[clayer, c + 1, 3], zspread[clayer, c - 1, 3]),
                (up, down, h, h_down, n_up, n_down),
                (ahead, behind, zspread[clayer, c, 2], zspread[clayer - 1, c, 2], zspread[clayer + 1, c, 3], zspread[clayer - 1, c, 3]),
            )
            z2[side, x] = v + flux(diff_ref[...], v, n, parts)

    def finish(x):
        for y in range(8):
            below, above = z2[0, x, y : y + 1, :], z2[1, x, y : y + 1, :]
            v, change = column(v2, 1, x, y, below, above, zcoef(1, x, y), zcoef(4, x, y))
            result[x, y] = 0.5 * v1[2 + x, 2 + y] + 0.5 * (v + change)

    def widen_column(x, y, tile, at):
        for c, value in enumerate(widen(tile, at)):
            spread[2 + x, 2 + y, c] = value

    def widen_layer(clayer, x, tile, at):
        for c, value in enumerate(widen(tile, at)):
            zspread[clayer, 1 + x, c] = value

    def widen_plane(side, places, x, edges, at):
        for i, place_x in enumerate(places):
            tile = kx_in[side, i]
            for y in range(8):
                widen_column(place_x, y, tile, y)
        widen_column(x, -1, ke_in[edges], 7)
        widen_column(x, 8, ke_in[edges + 1], 0)
        widen_layer(1, x, ke_in[4 + edges], at)
        widen_layer(4, x, ke_in[5 + edges], at)

    def widen_sides():
        for side, i, y in ((0, 0, -2), (0, 1, -1), (1, 0, 8), (1, 1, 9)):
            tile = ky_in[side, i]
            for x in range(8):
                widen_column(x, y, tile, x)
        for side, i, clayer in ((0, 0, 0), (0, 1, 1), (1, 0, 4), (1, 1, 5)):
            tile = kz_in[side, i]
            for x in range(8):
                widen_layer(clayer, x, tile, x)
        for i in range(4):
            for c, value in enumerate(widen(kyz_in[i], 0)):
                yzspread[i, c] = value

    def store(i, x, n):
        copy = pltpu.make_async_copy(result.at[pl.ds(x, n)], out.at[pl.ds(x, n)], out_sem.at[i])
        copy.start()
        return copy

    ky[...] = jnp.zeros_like(ky)
    kz[...] = jnp.zeros_like(kz)
    for i in (6, 7, 8):
        loads[i].wait()

    def two_planes(level):
        own_coefficients(2 * level - 2)
        own_coefficients(2 * level - 1)

    first_along = lax.axis_index("gx") == 0
    others = jnp.logical_not(first_along)

    def leading(lo, hi):
        pl.when(first_along)(lambda: chemistry(0, 4, lo, hi, two_planes))
        pl.when(others)(lambda: chemistry(3, 1, lo, hi, two_planes))

    def remaining():
        loads[5].wait()
        chemistry(0, 3, 1, MAX_SUB)

    pl.when(first_along)(loads[5].wait)
    leading(1, 2)
    pl.semaphore_wait(barrier, len(GREETED))
    for steps in AHEAD:
        pl.semaphore_signal(entry_sem, inc=1, device_id=toward(steps), device_id_type=MESH)
    leading(3, MAX_SUB)
    each(6, 8, lambda x: pack_z(v1, 2, zp, x))
    r_plus = start(send_plus(v1, zp, zf))
    k_plus, k_minus, k_side = send_coefficients()

    pl.when(others)(remaining)
    each(0, 6, lambda x: pack_z(v1, 2, zp, x))
    pack_yz(v1, 2, yzp)
    r_side = start(send_side(v1, zp, zf, yzp, yz))
    r_minus = send_minus(v1, zp, zf)

    def send_back():
        pl.semaphore_wait(entry_sem, len(AHEAD))
        start(k_minus)
        start(r_minus)

    pl.when(others)(send_back)

    for copy in k_side:
        copy.wait_recv()
    widen_sides()
    for copy in r_side:
        copy.wait_recv()
    each(1, 7, first_plane)
    each(1, 7, first_rim)
    each(2, 6, finish)
    stored = [store(0, 2, 4)]
    for copy in k_minus:
        copy.wait_recv()
    widen_plane(1, (8, 9), 8, 2, 0)
    for copy in r_minus:
        copy.wait_recv()
    each(7, 9, first_plane)
    first_rim(7)
    each(6, 8, finish)
    stored.append(store(1, 6, 2))

    pl.when(first_along)(send_back)
    for copy in k_plus:
        copy.wait_recv()
    widen_plane(0, (-2, -1), -1, 0, 7)
    for copy in r_plus:
        copy.wait_recv()
    first_plane(-1)
    first_plane(0)
    first_rim(0)
    each(0, 2, finish)
    stored.append(store(2, 0, 2))
    for copy in used:
        copy.wait_send()
    for copy in stored:
        copy.wait()


def shards(sizes, species, substeps, reactants, products, rate_const, velocity, viscosity, diffusivity):
    hbm = pl.BlockSpec(memory_space=pltpu.HBM)
    messages = 36
    return pl.pallas_call(
        functools.partial(kernel, sizes),
        out_shape=jax.ShapeDtypeStruct(species.shape, F32),
        in_specs=[hbm] * 8,
        out_specs=hbm,
        scratch_shapes=[
            pltpu.VMEM((1024, 256), jnp.int32),
            pltpu.VMEM((1024, 256), jnp.int32),
            pltpu.SMEM((4,), jnp.int32),
            pltpu.VMEM((1, 1024), F32),
            pltpu.VMEM((4, 8, 8, 8), F32),
            pltpu.VMEM((1, 256), F32),
            pltpu.VMEM((1024, 512), BF16),
            pltpu.VMEM((1024, 512), BF16),
            pltpu.VMEM((12, 12, 8, 256), F32),
            pltpu.VMEM((10, 10, 8, 256), F32),
            pltpu.VMEM((4, 8, 8, 256), F32),
            pltpu.VMEM((4, 10, 8, 256), F32),
            pltpu.VMEM((4, 8, 256), F32),
            pltpu.VMEM((4, 8, 256), F32),
            pltpu.VMEM((2, 8, 8, 256), F32),
            pltpu.VMEM((8, 8, 8, 128), F32),
            pltpu.VMEM((4, 8, 8, 128), F32),
            pltpu.VMEM((8, 8, 128), F32),
            pltpu.VMEM((8, 8, 128), F32),
            pltpu.VMEM((4, 8, 128), F32),
            pltpu.VMEM((4, 8, 128), F32),
            pltpu.VMEM((2, 2, 8, 128), F32),
            pltpu.VMEM((2, 2, 8, 128), F32),
            pltpu.VMEM((2, 2, 8, 128), F32),
            pltpu.VMEM((8, 8, 128), F32),
            pltpu.VMEM((4, 8, 128), F32),
            pltpu.VMEM((12, 12, 4, 8, 128), F32),
            pltpu.VMEM((6, 10, 4, 8, 128), F32),
            pltpu.VMEM((4, 4, 8, 128), F32),
            pltpu.VMEM((8, 8, 8, 256), F32),
            pltpu.SemaphoreType.DMA((9,)),
            pltpu.SemaphoreType.DMA((3,)),
            pltpu.SemaphoreType.DMA((messages,)),
            pltpu.SemaphoreType.DMA((messages,)),
            pltpu.SemaphoreType.REGULAR,
        ],
        compiler_params=pltpu.CompilerParams(
            collective_id=0, has_side_effects=True, vmem_limit_bytes=63 * 2**20
        ),
    )(
        species,
        reactants,
        products,
        substeps.reshape(-1),
        rate_const.reshape(1, -1),
        velocity,
        viscosity,
        diffusivity.reshape(1, -1),
    )


def solution(mesh):
    return jax.shard_map(
        functools.partial(shards, dict(mesh.shape)),
        mesh=mesh,
        in_specs=(
            P("gx", "gy", "gz", None),
            P("gx", "gy", "gz"),
            P(),
            P(),
            P(),
            P(None, "gx", "gy", "gz"),
            P("gx", "gy", "gz"),
            P(),
        ),
        out_specs=P("gx", "gy", "gz", None),
        check_vma=False,
    )
```
